512 devices in a mesh: dp: 8 (over x, core), view: 64 (over y, z).
Axes of the slice: x: 4, y: 8, z: 8, core: 2. Of those that a mesh axis runs over, the one named last changes fastest.
Arguments:
- queries: bfloat16 [8, 8192, 2048], P('dp', 'view')
- keys: bfloat16 [8, 8192, 2048], P('dp', 'view')
- values: bfloat16 [8, 8192, 2048], P('dp', 'view'), may hold values from -6 to 6
- out_grad: bfloat16 [8, 8192, 2048], P('dp', 'view'), may hold values from -6 to 6
- gain: float32 [16, 128], replicated, may hold values from 0.1 to 1.9
- tasks: int32 [8, 64, 2], P('dp', 'view'), may hold values 0 or 1
- bounds: int32 [8, 64, 2], P('dp', 'view'), may hold values from 0 to 128, as said below
Outputs:
- attended: bfloat16 [8, 8192, 2048], P('dp', 'view')
- query_grad: bfloat16 [8, 8192, 2048], P('dp', 'view')
- key_grad: bfloat16 [8, 8192, 2048], P('dp', 'view')
- value_grad: bfloat16 [8, 8192, 2048], P('dp', 'view')
- gain_grad: float32 [16, 128], replicated
The draws below stay inside these ranges and needn't reach their ends.
Inputs may be any that keep to these rules, and one draw needn't show every extreme that they name: bounds[.,.,0] lies in 0 to 31 and bounds[.,.,1] in 97 to 128.
All inputs are finite; a program needn't handle non-finite values. No bound on the sum of `tasks` on one device may be relied on, other than what follows from the above.
Results may differ from the reference program's by a relative error of at most 0.003.
The reference program's roundings to bfloat16 on the way count: a program that leaves them out, or rounds other values in their place, can miss the bound.
Values may be sent and summed in bfloat16 or wider, within the bound.
No kernel may reach another device: no remote copies, remote signals or barrier semaphores. Data moves between devices by JAX's collectives and lax.ppermute only.
A program may use at most 64 MiB of HBM per device.

```python
import jax
import jax.numpy as jnp
from jax import lax

HEADS = 16
HEAD_DIM = 128
S_DEV = 128
REACH = 1
VIEW_TOKENS = 8192
WIDTH = 2048
N_DP = 8
N_VIEW = 64


def shared_field(key):
    return jax.random.normal(key, (N_DP, VIEW_TOKENS, WIDTH), jnp.float32)


def draw_keys(key, part):
    base = shared_field(key)
    return base.astype(jnp.bfloat16)


def draw_queries(key, part):
    key = jax.random.fold_in(key, 12)
    own = jax.random.normal(key, (N_DP, VIEW_TOKENS, WIDTH), jnp.float32)
    return own.astype(jnp.bfloat16)


def draw_bounds(key, part):
    key = jax.random.fold_in(key, 13)
    first_key, last_key = jax.random.split(key)
    first = jax.random.randint(first_key, (N_DP, N_VIEW, 1), 0, S_DEV // 4)
    last = S_DEV - jax.random.randint(last_key, (N_DP, N_VIEW, 1), 0, S_DEV // 4)
    return jnp.concatenate([first, last], axis=2).astype(jnp.int32)


def place_ends(values, stream_key, low, top_value):
    dims = values.shape
    index_at = [jax.random.randint(jax.random.fold_in(stream_key, axis), (), 0, dims[axis]) for axis in range(len(dims))]
    values = values.at[tuple(index_at)].set(low)
    longest = dims.index(max(dims))
    index_at[longest] = (index_at[longest] + 1) % dims[longest]
    return values.at[tuple(index_at)].set(top_value)


def levels(own_key, shape, cuts, least, high):
    level = 1.0
    for axis_at, parts in cuts:
        heights = jax.random.uniform(jax.random.fold_in(jax.random.fold_in(own_key, 6), axis_at), (parts,), jnp.float32, least / len(cuts), high / len(cuts))
        level = level * jnp.repeat(jnp.exp(heights), shape[axis_at] // parts).reshape((-1,) + (1,) * (len(shape) - 1 - axis_at))
    return level


def scatter_about(key, dims, scale, most, shards=(), held_as=jnp.bfloat16):
    level = levels(key, dims, shards, -0.22, 0.18) if shards else 1.0
    array = jax.random.normal(key, dims, jnp.float32) * scale * level
    return jnp.minimum(jnp.maximum(array, -most), most).astype(held_as)


def setup_inputs(seed: int = 0) -> dict:
    splits = jax.random.split(jax.random.key(seed), 8)
    return {
        "queries": draw_queries(jax.random.fold_in(splits[7], 71), 0),
        "keys": draw_keys(jax.random.fold_in(splits[7], 71), 0),
        "values": scatter_about(splits[2], (N_DP, VIEW_TOKENS, WIDTH), 1.0, 6.0, ((0, 8), (1, 64))),
        "out_grad": scatter_about(splits[3], (N_DP, VIEW_TOKENS, WIDTH), 1.0, 6.0, ((0, 8), (1, 64))),
        "gain": jnp.clip(1.0 + 0.18 * jax.random.normal(splits[4], (HEADS, HEAD_DIM), jnp.float32), 0.1, 1.9),
        "tasks": place_ends((jax.random.randint(splits[5], (N_DP, N_VIEW, 2 * REACH), 0, 2) < 1).astype(jnp.int32), jax.random.fold_in(splits[5], 1), 0, 1),
        "bounds": draw_bounds(jax.random.fold_in(splits[7], 71), 0),
    }


OFFSETS = (-1, 1)

def strip_pass(q, gain, keys_all, values_all, live, dout):
    scale_r = lax.rsqrt(lax.optimization_barrier(jnp.mean(q * q, axis=-1)) + 1e-06)
    normed = (q * scale_r[..., None] * gain).astype(jnp.bfloat16)
    inv = 1.0 / jnp.sqrt(jnp.float32(HEAD_DIM))
    nf = normed.astype(jnp.float32)
    kf = keys_all.astype(jnp.float32)
    vf = values_all.astype(jnp.float32)
    df = dout.astype(jnp.float32)
    scores = jnp.einsum('qhd,khd->hqk', nf, kf) * inv
    scores = jnp.where(live[None, None, :], scores, jnp.float32(-1e+30))
    rowmax = lax.optimization_barrier(jnp.max(scores, axis=-1))
    expo = jnp.exp(scores - rowmax[..., None])
    total = lax.optimization_barrier(jnp.sum(expo, axis=-1))
    prob = expo / total[..., None]
    prob_b = prob.astype(jnp.bfloat16)
    pf = prob_b.astype(jnp.float32)
    attended = jnp.einsum('hqk,khd->qhd', pf, vf).astype(jnp.bfloat16)
    dprob = jnp.einsum('qhd,khd->hqk', df, vf)
    delta = lax.optimization_barrier(jnp.sum(prob * dprob, axis=-1))
    dscore = (prob * (dprob - delta[..., None])).astype(jnp.bfloat16)
    sf = dscore.astype(jnp.float32)
    dnormed = jnp.einsum('hqk,khd->qhd', sf, kf) * inv
    inner = lax.optimization_barrier(jnp.sum(q * gain * dnormed, axis=-1))
    r3 = scale_r * scale_r * scale_r
    qgrad = gain * scale_r[..., None] * dnormed - q * (r3 * inner / HEAD_DIM)[..., None]
    ggrad = lax.optimization_barrier(jnp.sum(q * scale_r[..., None] * dnormed, axis=0))
    kgrad = jnp.einsum('hqk,qhd->khd', sf, nf) * inv
    vgrad = jnp.einsum('hqk,qhd->khd', pf, df)
    return (attended, qgrad.astype(jnp.bfloat16), ggrad, kgrad, vgrad)

def group_pass(q, k, v, dout, tasks_row, bounds_row, gain):
    shape = (N_VIEW, S_DEV, HEADS, HEAD_DIM)
    q = q.reshape(shape).astype(jnp.float32)
    k = k.reshape(shape)
    v = v.reshape(shape)
    dout = dout.reshape(shape)
    rows = jnp.arange(S_DEV, dtype=jnp.int32)
    valid = (rows[None, :] >= bounds_row[:, 0:1]) & (rows[None, :] < bounds_row[:, 1:2])
    key_list = [k]
    value_list = [v]
    live_list = [valid]
    for idx, offset in enumerate(OFFSETS):
        key_list.append(jnp.roll(k, -offset, axis=0))
        value_list.append(jnp.roll(v, -offset, axis=0))
        live_list.append(jnp.roll(valid, -offset, axis=0) & (tasks_row[:, idx:idx + 1] > 0))
    keys_all = jnp.concatenate(key_list, axis=1)
    values_all = jnp.concatenate(value_list, axis=1)
    live = jnp.concatenate(live_list, axis=1)
    attended, qgrad, ggrad, kgrad, vgrad = jax.vmap(strip_pass, in_axes=(0, None, 0, 0, 0, 0))(q, gain, keys_all, values_all, live, dout)
    ktotal = kgrad[:, :S_DEV]
    vtotal = vgrad[:, :S_DEV]
    for idx, offset in enumerate(OFFSETS):
        lo = (idx + 1) * S_DEV
        ktotal = ktotal + jnp.roll(kgrad[:, lo:lo + S_DEV], offset, axis=0)
        vtotal = vtotal + jnp.roll(vgrad[:, lo:lo + S_DEV], offset, axis=0)
    flat = (VIEW_TOKENS, WIDTH)
    return (attended.reshape(flat), qgrad.reshape(flat), ktotal.astype(jnp.bfloat16).reshape(flat), vtotal.astype(jnp.bfloat16).reshape(flat), lax.optimization_barrier(jnp.sum(ggrad, axis=0)))

def reference(queries, keys, values, out_grad, gain, tasks, bounds):

    def one_group(items):
        return group_pass(items[0], items[1], items[2], items[3], items[4], items[5], gain)
    attended, qgrad, kgrad, vgrad, ggrad = lax.map(one_group, (queries, keys, values, out_grad, tasks, bounds))
    return (attended, qgrad, kgrad, vgrad, lax.optimization_barrier(jnp.sum(ggrad, axis=0)))
```

```python
import jax
import jax.numpy as jnp
from jax import lax
from jax.experimental import pallas as pl
from jax.experimental.pallas import tpu as pltpu
from jax.sharding import PartitionSpec as P

HEAD_DIM = 128
DEAD = -1e30
EPS = 1e-06
PER_STEP = 4
STATS = 4
MASK_ROWS = 16
RING = 8
NT = (((1,), (1,)), ((), ()))
NN = (((1,), (0,)), ((), ()))


def dot(a, b, dims):
    return lax.dot_general(a, b, dims, preferred_element_type=jnp.float32)


def shifted(array, axis, by):
    count = lax.axis_size(axis)
    return lax.ppermute(array, axis, [(i, (i + by) % count) for i in range(count)])


def columns_of(i):
    return slice(i * HEAD_DIM, (i + 1) * HEAD_DIM)


def head(ref, i):
    return ref[0, :, columns_of(i)]


def heads_of(refs, i):
    return jnp.concatenate([head(r, i) for r in refs], axis=0)


def pack_kernel(own_ref, k_ref, v_ref, out_ref):
    strip, width = k_ref.shape[1:]
    out_ref[0, :strip, :] = k_ref[0]
    out_ref[0, strip : 2 * strip, :] = v_ref[0]
    at = lax.broadcasted_iota(jnp.int32, (MASK_ROWS, width), 1)
    valid = (at >= own_ref[0]) & (at < own_ref[1])
    out_ref[0, 2 * strip :, :] = valid.astype(jnp.float32).astype(jnp.bfloat16)


def norm_kernel(q_ref, do_ref, gain_ref, out_ref):
    step = pl.program_id(0)
    strip = q_ref.shape[1]
    for i in range(PER_STEP):
        q = head(q_ref, i).astype(jnp.float32)
        gain = gain_ref[pl.ds(step * PER_STEP + i, 1), :]
        scale = lax.rsqrt(jnp.mean(q * q, axis=-1, keepdims=True) + EPS)
        out_ref[0, :strip, columns_of(i)] = (q * scale * gain).astype(jnp.bfloat16)
    out_ref[0, strip:, :] = do_ref[0]


def query_kernel(
    tasks_ref, own_ref,
    q_ref, n_ref, do_ref, k0_ref, v0_ref, k1_ref, v1_ref, m1_ref, k2_ref, v2_ref, m2_ref, gain_ref,
    att_ref, qgrad_ref, gpart_ref, stats_ref,
):
    step = pl.program_id(0)
    strip = q_ref.shape[1]
    inv = 1.0 / (HEAD_DIM**0.5)
    at = lax.broadcasted_iota(jnp.int32, (1, strip), 1)
    flags = (tasks_ref[0] > 0).astype(jnp.float32), (tasks_ref[1] > 0).astype(jnp.float32)
    own = ((at >= own_ref[0]) & (at < own_ref[1])).astype(jnp.float32)
    left = m1_ref[0, 0:1, :].astype(jnp.float32) * flags[0]
    right = m2_ref[0, 0:1, :].astype(jnp.float32) * flags[1]
    live = jnp.concatenate([own, left, right], axis=1) > 0.5
    lane = lax.broadcasted_iota(jnp.int32, (strip, 128), 1)
    columns = jnp.full((strip, 128), flags[0] + 2.0 * flags[1], jnp.float32)
    keys, values = (k0_ref, k1_ref, k2_ref), (v0_ref, v1_ref, v2_ref)
    each = range(PER_STEP)
    scores = [dot(head(n_ref, i), heads_of(keys, i), NT) for i in each]
    dprob = [dot(head(do_ref, i), heads_of(values, i), NT) for i in each]
    prob_b, dscore = [], []
    for i in each:
        masked = jnp.where(live, scores[i] * inv, DEAD)
        rowmax = jnp.max(masked, axis=-1, keepdims=True)
        expo = jnp.exp(masked - rowmax)
        share = 1.0 / jnp.sum(expo, axis=-1, keepdims=True)
        prob = expo * share
        delta = jnp.sum(prob * dprob[i], axis=-1, keepdims=True)
        prob_b.append(prob.astype(jnp.bfloat16))
        dscore.append((prob * (dprob[i] - delta)).astype(jnp.bfloat16))
        for j, stat in enumerate((rowmax, share, delta)):
            columns = jnp.where(lane == i * STATS + j, stat, columns)
    dnormed = [dot(dscore[i], heads_of(keys, i), NN) * inv for i in each]
    for i in each:
        att_ref[0, :, columns_of(i)] = dot(prob_b[i], heads_of(values, i), NN).astype(jnp.bfloat16)
    for i in each:
        row = pl.ds(step * PER_STEP + i, 1)
        gain = gain_ref[row, :]
        q = head(q_ref, i).astype(jnp.float32)
        scale = lax.rsqrt(jnp.mean(q * q, axis=-1, keepdims=True) + EPS)
        inner = jnp.sum(q * gain * dnormed[i], axis=-1, keepdims=True)
        cubed = scale * scale * scale
        qgrad = gain * scale * dnormed[i] - q * (cubed * inner * (1.0 / HEAD_DIM))
        qgrad_ref[0, :, columns_of(i)] = qgrad.astype(jnp.bfloat16)
        gpart_ref[row, :] = jnp.sum(q * scale * dnormed[i], axis=0, keepdims=True)
    stats_ref[...] = columns.T[: PER_STEP * STATS, :]


def key_kernel(
    own_ref,
    k_ref, v_ref, n0_ref, d0_ref, n1_ref, d1_ref, n2_ref, d2_ref, s0_ref, s1_ref, s2_ref,
    kgrad_ref, vgrad_ref,
):
    strip = k_ref.shape[1]
    inv = 1.0 / (HEAD_DIM**0.5)
    at = lax.broadcasted_iota(jnp.int32, (strip, 1), 0)
    valid = (at >= own_ref[0]) & (at < own_ref[1])
    left = s1_ref[3:4, :] >= 1.5
    right_flags = s2_ref[3:4, :]
    right = (right_flags == 1.0) | (right_flags == 3.0)
    live = jnp.concatenate(
        [jnp.broadcast_to(valid, (strip, strip)), valid & left, valid & right], axis=1
    )
    normed, dout = (n0_ref, n1_ref, n2_ref), (d0_ref, d1_ref, d2_ref)
    each = range(PER_STEP)
    scores = [dot(head(k_ref, i), heads_of(normed, i), NT) for i in each]
    dprob = [dot(head(v_ref, i), heads_of(dout, i), NT) for i in each]
    prob_b, dscore = [], []
    for i in each:
        rowmax, share, delta = (
            jnp.concatenate(
                [r[i * STATS + j : i * STATS + j + 1, :] for r in (s0_ref, s1_ref, s2_ref)], axis=1
            )
            for j in range(3)
        )
        masked = jnp.where(live, scores[i] * inv, DEAD)
        prob = jnp.exp(masked - rowmax) * share
        prob_b.append(prob.astype(jnp.bfloat16))
        dscore.append((prob * (dprob[i] - delta)).astype(jnp.bfloat16))
    for i in each:
        vgrad_ref[0, :, columns_of(i)] = dot(prob_b[i], heads_of(dout, i), NN).astype(jnp.bfloat16)
    for i in each:
        kgrad = dot(dscore[i], heads_of(normed, i), NN) * inv
        kgrad_ref[0, :, columns_of(i)] = kgrad.astype(jnp.bfloat16)


def total_over(part, axis, groups=None):
    count = lax.axis_size(axis) if groups is None else len(groups[0])
    if count == 1:
        return part
    blocks = jnp.broadcast_to(part[None], (count, *part.shape))
    blocks = lax.all_to_all(blocks, axis, 0, 0, axis_index_groups=groups, tiled=True)
    return jnp.sum(blocks, axis=0)


def on_device(queries, keys, values, out_grad, gain, tasks, bounds):
    _, strip, width = queries.shape
    heads = width // HEAD_DIM
    steps = heads // PER_STEP
    cols = PER_STEP * HEAD_DIM
    first = pl.BlockSpec((1, strip, cols), lambda i: (0, 0, i))
    second = pl.BlockSpec((1, strip, cols), lambda i: (0, 1, i))
    mask = pl.BlockSpec((1, MASK_ROWS, strip), lambda i: (0, 2 * strip // MASK_ROWS, 0))
    whole = pl.BlockSpec((heads, HEAD_DIM), lambda i: (0, 0))
    stat_block = pl.BlockSpec((PER_STEP * STATS, strip), lambda i: (i, 0))
    scalars = pl.BlockSpec(memory_space=pltpu.SMEM)
    wide = jax.ShapeDtypeStruct(queries.shape, jnp.bfloat16)
    params = pltpu.CompilerParams(vmem_limit_bytes=56 * 1024 * 1024)
    own_bounds, own_tasks = bounds.reshape(2), tasks.reshape(2)

    rows = 2 * strip + MASK_ROWS
    packed = pl.pallas_call(
        pack_kernel,
        grid=(steps,),
        in_specs=[scalars, first, first],
        out_specs=pl.BlockSpec((1, rows, cols), lambda i: (0, 0, i)),
        out_shape=jax.ShapeDtypeStruct((1, rows, width), jnp.bfloat16),
        compiler_params=params,
    )(own_bounds, keys, values)
    kv_left, kv_right = shifted(packed, "view", 1), shifted(packed, "view", -1)
    nd = pl.pallas_call(
        norm_kernel,
        grid=(steps,),
        in_specs=[first, first, whole],
        out_specs=pl.BlockSpec((1, 2 * strip, cols), lambda i: (0, 0, i)),
        out_shape=jax.ShapeDtypeStruct((1, 2 * strip, width), jnp.bfloat16),
        compiler_params=params,
    )(queries, out_grad, gain)
    nd_left, nd_right = shifted(nd, "view", 1), shifted(nd, "view", -1)

    mac = strip * strip * width
    attended, qgrad, gain_part, stats = pl.pallas_call(
        query_kernel,
        grid=(steps,),
        in_specs=[scalars] * 2 + [first] * 5 + [first, second, mask] * 2 + [whole],
        out_specs=[first, first, whole, stat_block],
        out_shape=[
            wide,
            wide,
            jax.ShapeDtypeStruct((heads, HEAD_DIM), jnp.float32),
            jax.ShapeDtypeStruct((heads * STATS, strip), jnp.float32),
        ],
        compiler_params=params,
        cost_estimate=pl.CostEstimate(
            flops=24 * mac, bytes_accessed=22 * strip * width, transcendentals=3 * heads * strip * strip
        ),
    )(
        own_tasks, own_bounds, queries, nd, out_grad, keys, values,
        kv_left, kv_left, kv_left, kv_right, kv_right, kv_right, gain,
    )
    s_left, s_right = shifted(stats, "view", 1), shifted(stats, "view", -1)

    count = lax.axis_size("view")
    ring = RING if count % RING == 0 else count
    across = [[y * ring + z for y in range(count // ring)] for z in range(ring)]
    along = [[y * ring + z for z in range(ring)] for y in range(count // ring)]
    gain_grad = total_over(gain_part, "dp")
    gain_grad = total_over(gain_grad, "view", across)
    gain_grad = total_over(gain_grad, "view", along)

    kgrad, vgrad = pl.pallas_call(
        key_kernel,
        grid=(steps,),
        in_specs=[scalars] + [first] * 2 + [first, second] * 3 + [stat_block] * 3,
        out_specs=[first, first],
        out_shape=[wide, wide],
        compiler_params=params,
        cost_estimate=pl.CostEstimate(
            flops=24 * mac, bytes_accessed=20 * strip * width, transcendentals=3 * heads * strip * strip
        ),
    )(
        own_bounds, keys, values, nd, nd, nd_left, nd_left, nd_right, nd_right, stats, s_left, s_right
    )
    return attended, qgrad, kgrad, vgrad, gain_grad


def solution(mesh):
    rows = P("dp", "view", None)
    return jax.shard_map(
        on_device,
        mesh=mesh,
        in_specs=(rows, rows, rows, rows, P(), rows, rows),
        out_specs=(rows, rows, rows, rows, P()),
        check_vma=False,
    )
```

```python
import functools

import jax
import jax.numpy as jnp
from jax import lax
from jax.experimental import pallas as pl
from jax.experimental.pallas import tpu as pltpu
from jax.sharding import PartitionSpec as P

HEAD_DIM = 128
DEAD = -1e30
EPS = 1e-06
PER_STEP = 4
STATS = 4
MASK_ROWS = 16
RING = 8
NT = (((1,), (1,)), ((), ()))
NN = (((1,), (0,)), ((), ()))


def dot(a, b, dims):
    return lax.dot_general(a, b, dims, preferred_element_type=jnp.float32)


def shifted(array, axis, by):
    count = lax.axis_size(axis)
    return lax.ppermute(array, axis, [(i, (i + by) % count) for i in range(count)])


def columns_of(i):
    return slice(i * HEAD_DIM, (i + 1) * HEAD_DIM)


def head(ref, i):
    return ref[0, :, columns_of(i)]


def heads_of(refs, i):
    return jnp.concatenate([head(r, i) for r in refs], axis=0)


def pack_kernel(own_ref, k_ref, v_ref, out_ref):
    strip, width = k_ref.shape[1:]
    out_ref[0, :strip, :] = k_ref[0]
    out_ref[0, strip : 2 * strip, :] = v_ref[0]
    at = lax.broadcasted_iota(jnp.int32, (MASK_ROWS, width), 1)
    valid = (at >= own_ref[0]) & (at < own_ref[1])
    out_ref[0, 2 * strip :, :] = valid.astype(jnp.float32).astype(jnp.bfloat16)


def prep_kernel(k_ref, v_ref, q_ref, do_ref, gain_ref, kv_ref, nd_ref):
    step = pl.program_id(0)
    strip = k_ref.shape[1]
    kv_ref[0, :strip, :] = k_ref[0]
    kv_ref[0, strip:, :] = v_ref[0]
    for i in range(PER_STEP):
        q = head(q_ref, i).astype(jnp.float32)
        gain = gain_ref[pl.ds(step * PER_STEP + i, 1), :]
        scale = lax.rsqrt(jnp.mean(q * q, axis=-1, keepdims=True) + EPS)
        nd_ref[0, :strip, columns_of(i)] = (q * scale * gain).astype(jnp.bfloat16)
    nd_ref[0, strip:, :] = do_ref[0]


def query_kernel(
    start, tasks_ref, own_ref,
    q_ref, n_ref, do_ref, k0_ref, v0_ref, k1_ref, v1_ref, m1_ref, k2_ref, v2_ref, m2_ref, gain_ref,
    *rest,
):
    att_ref, qgrad_ref, stats_ref, gpart_ref = rest[-4:]
    if start:
        gpart_ref[:, :start, :] = jnp.broadcast_to(
            rest[3][...], (gpart_ref.shape[0], start, HEAD_DIM)
        )
    step = pl.program_id(0)
    strip = q_ref.shape[1]
    inv = 1.0 / (HEAD_DIM**0.5)
    at = lax.broadcasted_iota(jnp.int32, (1, strip), 1)
    flags = (tasks_ref[0] > 0).astype(jnp.float32), (tasks_ref[1] > 0).astype(jnp.float32)
    own = ((at >= own_ref[0]) & (at < own_ref[1])).astype(jnp.float32)
    left = m1_ref[0, 0:1, :].astype(jnp.float32) * flags[0]
    right = m2_ref[0, 0:1, :].astype(jnp.float32) * flags[1]
    live = jnp.concatenate([own, left, right], axis=1) > 0.5
    lane = lax.broadcasted_iota(jnp.int32, (strip, 128), 1)
    columns = jnp.full((strip, 128), flags[0] + 2.0 * flags[1], jnp.float32)
    keys, values = (k0_ref, k1_ref, k2_ref), (v0_ref, v1_ref, v2_ref)
    each = range(PER_STEP)
    scores = [dot(head(n_ref, i), heads_of(keys, i), NT) for i in each]
    dprob = [dot(head(do_ref, i), heads_of(values, i), NT) for i in each]
    prob_b, dscore = [], []
    for i in each:
        masked = jnp.where(live, scores[i] * inv, DEAD)
        rowmax = jnp.max(masked, axis=-1, keepdims=True)
        expo = jnp.exp(masked - rowmax)
        share = 1.0 / jnp.sum(expo, axis=-1, keepdims=True)
        prob = expo * share
        delta = jnp.sum(prob * dprob[i], axis=-1, keepdims=True)
        prob_b.append(prob.astype(jnp.bfloat16))
        dscore.append((prob * (dprob[i] - delta)).astype(jnp.bfloat16))
        for j, stat in enumerate((rowmax, share, delta)):
            columns = jnp.where(lane == i * STATS + j, stat, columns)
    dnormed = [dot(dscore[i], heads_of(keys, i), NN) * inv for i in each]
    for i in each:
        att_ref[0, :, columns_of(i)] = dot(prob_b[i], heads_of(values, i), NN).astype(jnp.bfloat16)
    for i in each:
        row = pl.ds(start + step * PER_STEP + i, 1)
        gain = gain_ref[row, :]
        q = head(q_ref, i).astype(jnp.float32)
        scale = lax.rsqrt(jnp.mean(q * q, axis=-1, keepdims=True) + EPS)
        inner = jnp.sum(q * gain * dnormed[i], axis=-1, keepdims=True)
        cubed = scale * scale * scale
        qgrad = gain * scale * dnormed[i] - q * (cubed * inner * (1.0 / HEAD_DIM))
        qgrad_ref[0, :, columns_of(i)] = qgrad.astype(jnp.bfloat16)
        part = jnp.sum(q * scale * dnormed[i], axis=0, keepdims=True)
        for j in range(gpart_ref.shape[0]):
            gpart_ref[j, row, :] = part
    stats_ref[...] = columns.T[: PER_STEP * STATS, :]


def key_kernel(
    own_ref,
    k_ref, v_ref, n0_ref, d0_ref, n1_ref, d1_ref, n2_ref, d2_ref, s0_ref, s1_ref, s2_ref,
    kgrad_ref, vgrad_ref,
):
    strip = k_ref.shape[1]
    inv = 1.0 / (HEAD_DIM**0.5)
    at = lax.broadcasted_iota(jnp.int32, (strip, 1), 0)
    valid = (at >= own_ref[0]) & (at < own_ref[1])
    left = s1_ref[3:4, :] >= 1.5
    right_flags = s2_ref[3:4, :]
    right = (right_flags == 1.0) | (right_flags == 3.0)
    live = jnp.concatenate(
        [jnp.broadcast_to(valid, (strip, strip)), valid & left, valid & right], axis=1
    )
    normed, dout = (n0_ref, n1_ref, n2_ref), (d0_ref, d1_ref, d2_ref)
    each = range(PER_STEP)
    scores = [dot(head(k_ref, i), heads_of(normed, i), NT) for i in each]
    dprob = [dot(head(v_ref, i), heads_of(dout, i), NT) for i in each]
    prob_b, dscore = [], []
    for i in each:
        rowmax, share, delta = (
            jnp.concatenate(
                [r[i * STATS + j : i * STATS + j + 1, :] for r in (s0_ref, s1_ref, s2_ref)], axis=1
            )
            for j in range(3)
        )
        masked = jnp.where(live, scores[i] * inv, DEAD)
        prob = jnp.exp(masked - rowmax) * share
        prob_b.append(prob.astype(jnp.bfloat16))
        dscore.append((prob * (dprob[i] - delta)).astype(jnp.bfloat16))
    for i in each:
        vgrad_ref[0, :, columns_of(i)] = dot(prob_b[i], heads_of(dout, i), NN).astype(jnp.bfloat16)
    for i in each:
        kgrad = dot(dscore[i], heads_of(normed, i), NN) * inv
        kgrad_ref[0, :, columns_of(i)] = kgrad.astype(jnp.bfloat16)


def total_over(blocks, axis, groups=None):
    if blocks.shape[0] > 1:
        blocks = lax.all_to_all(blocks, axis, 0, 0, axis_index_groups=groups, tiled=True)
    return jnp.sum(blocks, axis=0)


def copies(part, count):
    return jnp.broadcast_to(part[None], (count, *part.shape))


def tied(value, *others):
    return lax.optimization_barrier((value, *others))[0]


def on_device(queries, keys, values, out_grad, gain, tasks, bounds):
    _, strip, width = queries.shape
    heads = width // HEAD_DIM
    steps = heads // PER_STEP
    cols = PER_STEP * HEAD_DIM
    halves = 2
    per_half = steps // halves
    n_dp = lax.axis_size("dp")
    count = lax.axis_size("view")
    ring = RING if count % RING == 0 else count

    def block(row, at=0, of=cols):
        return pl.BlockSpec((1, strip, of), lambda i: (0, row, at + i))

    whole = pl.BlockSpec((heads, HEAD_DIM), lambda i: (0, 0))
    scalars = pl.BlockSpec(memory_space=pltpu.SMEM)
    anywhere = pl.BlockSpec(memory_space=pl.ANY)
    wide = jax.ShapeDtypeStruct(queries.shape, jnp.bfloat16)
    own_bounds, own_tasks = bounds.reshape(2), tasks.reshape(2)
    mac = strip * strip * width

    def call(kernel, grid, in_specs, out_specs, out_shape, cost=0, aliases=None):
        return pl.pallas_call(
            kernel,
            grid=(grid,),
            in_specs=in_specs,
            out_specs=out_specs,
            out_shape=out_shape,
            input_output_aliases=aliases or {},
            name=(kernel.func if isinstance(kernel, functools.partial) else kernel).__name__,
            compiler_params=pltpu.CompilerParams(vmem_limit_bytes=63 * 1024 * 1024),
            cost_estimate=pl.CostEstimate(flops=cost * mac, bytes_accessed=8 * strip * width, transcendentals=0),
        )

    rows = 2 * strip + MASK_ROWS
    kv0 = call(
        pack_kernel,
        per_half,
        [scalars, block(0), block(0)],
        pl.BlockSpec((1, rows, cols), lambda i: (0, 0, i)),
        jax.ShapeDtypeStruct((1, rows, width // halves), jnp.bfloat16),
    )(own_bounds, keys, values)
    kv0_left, kv0_right = shifted(kv0, "view", 1), shifted(kv0, "view", -1)

    thin = cols // halves
    kv1, nd = call(
        prep_kernel,
        steps,
        [block(0, steps, thin), block(0, steps, thin), block(0), block(0), whole],
        [
            pl.BlockSpec((1, 2 * strip, thin), lambda i: (0, 0, i)),
            pl.BlockSpec((1, 2 * strip, cols), lambda i: (0, 0, i)),
        ],
        [
            jax.ShapeDtypeStruct((1, 2 * strip, width // halves), jnp.bfloat16),
            jax.ShapeDtypeStruct((1, 2 * strip, width), jnp.bfloat16),
        ],
        cost=140,
    )(keys, values, queries, out_grad, gain)
    kv1_left, kv1_right = shifted(kv1, "view", 1), shifted(kv1, "view", -1)

    def query_side(half, left, right, before):
        at = half * per_half
        mask = pl.BlockSpec((1, MASK_ROWS, strip), lambda i: (0, 2 * strip // MASK_ROWS, 0))
        near = [block(0), block(1), mask]
        count, per = (1, heads // halves) if half == 0 else (n_dp, heads)
        return call(
            functools.partial(query_kernel, at * PER_STEP),
            per_half,
            [scalars] * 2 + [block(0, at)] * 5 + near * 2 + [whole]
            + [anywhere] * (3 if half else 0)
            + [pl.BlockSpec((1, heads // halves, HEAD_DIM), lambda i: (0, 0, 0))] * (1 if half else 0),
            [
                block(0, at),
                block(0, at),
                pl.BlockSpec((PER_STEP * STATS, strip), lambda i: (at + i, 0)),
                pl.BlockSpec((count, per, HEAD_DIM), lambda i: (0, 0, 0)),
            ],
            [
                wide,
                wide,
                jax.ShapeDtypeStruct((heads * STATS, strip), jnp.float32),
                jax.ShapeDtypeStruct((count, per, HEAD_DIM), jnp.float32),
            ],
            cost=3000,
            aliases={14: 0, 15: 1, 16: 2} if half else None,
        )(
            own_tasks, own_bounds, queries, nd, out_grad, keys, values,
            left, left, kv0_left, right, right, kv0_right, gain, *before,
        )

    early = query_side(0, kv0_left, kv0_right, ())
    attended, qgrad, stats, gain_parts = query_side(1, kv1_left, kv1_right, early)
    nd_sent = nd
    nd_left, nd_right = shifted(nd_sent, "view", 1), shifted(nd_sent, "view", -1)
    s_left, s_right = shifted(stats, "view", 1), shifted(stats, "view", -1)

    across = [[y * ring + z for y in range(count // ring)] for z in range(ring)]
    along = [[y * ring + z for z in range(ring)] for y in range(count // ring)]
    gain_grad = total_over(gain_parts, "dp")
    gain_grad = total_over(copies(gain_grad, count // ring), "view", across)

    own = [block(0), block(1)]
    stat_block = pl.BlockSpec((PER_STEP * STATS, strip), lambda i: (i, 0))
    kgrad, vgrad = call(
        key_kernel,
        steps,
        [scalars] + [block(0)] * 2 + own * 3 + [stat_block] * 3,
        [block(0)] * 2,
        [wide, wide],
        cost=30,
    )(
        own_bounds, keys, values, nd, nd, nd_left, nd_left, nd_right, nd_right, stats, s_left, s_right
    )
    blocks = lax.all_to_all(copies(gain_grad, ring), "view", 0, 0, axis_index_groups=along, tiled=True)
    gain_grad = jnp.sum(tied(blocks, kgrad), axis=0)
    return attended, qgrad, kgrad, vgrad, gain_grad


def solution(mesh):
    rows = P("dp", "view", None)
    return jax.shard_map(
        on_device,
        mesh=mesh,
        in_specs=(rows, rows, rows, rows, P(), rows, rows),
        out_specs=(rows, rows, rows, rows, P()),
        check_vma=False,
    )
```

```python
import functools

import jax
import jax.numpy as jnp
from jax import lax
from jax.experimental import pallas as pl
from jax.experimental.pallas import tpu as pltpu
from jax.sharding import PartitionSpec as P

HEAD_DIM = 128
DEAD = -1e30
EPS = 1e-06
PER_STEP = 4
STATS = 4
MASK_ROWS = 16
PREP_STEPS = 2
SHARE = 2
RING = 8
NT = (((1,), (1,)), ((), ()))
NN = (((1,), (0,)), ((), ()))


def dot(a, b, dims):
    return lax.dot_general(a, b, dims, preferred_element_type=jnp.float32)


def shifted(array, axis, by):
    count = lax.axis_size(axis)
    return lax.ppermute(array, axis, [(i, (i + by) % count) for i in range(count)])


def columns_of(i):
    return slice(i * HEAD_DIM, (i + 1) * HEAD_DIM)


def head(ref, i):
    return ref[0, :, columns_of(i)]


def heads_of(refs, i):
    return jnp.concatenate([head(r, i) for r in refs], axis=0)


def pack_kernel(own_ref, k_ref, v_ref, out_ref):
    strip, width = k_ref.shape[1:]
    out_ref[0, :strip, :] = k_ref[0]
    out_ref[0, strip : 2 * strip, :] = v_ref[0]
    at = lax.broadcasted_iota(jnp.int32, (MASK_ROWS, width), 1) % strip
    valid = (at >= own_ref[0]) & (at < own_ref[1])
    out_ref[0, 2 * strip :, :] = valid.astype(jnp.float32).astype(jnp.bfloat16)


def prep_kernel(k_ref, v_ref, q_ref, do_ref, gain_ref, kv_ref, nd_ref):
    step = pl.program_id(0)
    strip = k_ref.shape[1]
    kv_ref[0, :strip, :] = k_ref[0]
    kv_ref[0, strip:, :] = v_ref[0]
    count = q_ref.shape[2] // HEAD_DIM
    for i in range(count):
        q = head(q_ref, i).astype(jnp.float32)
        gain = gain_ref[pl.ds(step * count + i, 1), :]
        scale = lax.rsqrt(jnp.mean(q * q, axis=-1, keepdims=True) + EPS)
        nd_ref[0, :strip, columns_of(i)] = (q * scale * gain).astype(jnp.bfloat16)
    nd_ref[0, strip:, :] = do_ref[0]


def query_kernel(
    start, tasks_ref, own_ref,
    q_ref, n_ref, do_ref, k0_ref, v0_ref, k1_ref, v1_ref, m1_ref, k2_ref, v2_ref, m2_ref, gain_ref,
    *rest,
):
    att_ref, qgrad_ref, stats_ref, gpart_ref = rest[-4:]
    if start:
        gpart_ref[:, :start, :] = jnp.broadcast_to(
            rest[3][...], (gpart_ref.shape[0], start, HEAD_DIM)
        )
    step = pl.program_id(0)
    strip = q_ref.shape[1]
    inv = 1.0 / (HEAD_DIM**0.5)
    at = lax.broadcasted_iota(jnp.int32, (1, strip), 1)
    flags = (tasks_ref[0] > 0).astype(jnp.float32), (tasks_ref[1] > 0).astype(jnp.float32)
    own = ((at >= own_ref[0]) & (at < own_ref[1])).astype(jnp.float32)
    left = m1_ref[0, 0:1, :].astype(jnp.float32) * flags[0]
    right = m2_ref[0, 0:1, :].astype(jnp.float32) * flags[1]
    live = jnp.concatenate([own, left, right], axis=1) > 0.5
    lane = lax.broadcasted_iota(jnp.int32, (strip, 128), 1)
    columns = jnp.full((strip, 128), flags[0] + 2.0 * flags[1], jnp.float32)
    keys, values = (k0_ref, k1_ref, k2_ref), (v0_ref, v1_ref, v2_ref)
    each = range(PER_STEP)
    scores = [dot(head(n_ref, i), heads_of(keys, i), NT) for i in each]
    dprob = [dot(head(do_ref, i), heads_of(values, i), NT) for i in each]
    prob_b, dscore = [], []
    for i in each:
        masked = jnp.where(live, scores[i] * inv, DEAD)
        rowmax = jnp.max(masked, axis=-1, keepdims=True)
        expo = jnp.exp(masked - rowmax)
        share = 1.0 / jnp.sum(expo, axis=-1, keepdims=True)
        prob = expo * share
        delta = jnp.sum(prob * dprob[i], axis=-1, keepdims=True)
        prob_b.append(prob.astype(jnp.bfloat16))
        dscore.append((prob * (dprob[i] - delta)).astype(jnp.bfloat16))
        for j, stat in enumerate((rowmax, share, delta)):
            columns = jnp.where(lane == i * STATS + j, stat, columns)
    dnormed = [dot(dscore[i], heads_of(keys, i), NN) * inv for i in each]
    for i in each:
        att_ref[0, :, columns_of(i)] = dot(prob_b[i], heads_of(values, i), NN).astype(jnp.bfloat16)
    for i in each:
        row = pl.ds(start + step * PER_STEP + i, 1)
        gain = gain_ref[row, :]
        q = head(q_ref, i).astype(jnp.float32)
        scale = lax.rsqrt(jnp.mean(q * q, axis=-1, keepdims=True) + EPS)
        inner = jnp.sum(q * gain * dnormed[i], axis=-1, keepdims=True)
        cubed = scale * scale * scale
        qgrad = gain * scale * dnormed[i] - q * (cubed * inner * (1.0 / HEAD_DIM))
        qgrad_ref[0, :, columns_of(i)] = qgrad.astype(jnp.bfloat16)
        part = jnp.sum(q * scale * dnormed[i], axis=0, keepdims=True)
        for j in range(gpart_ref.shape[0]):
            gpart_ref[j, row, :] = part
    stats_ref[...] = columns.T[: PER_STEP * STATS, :]


def key_kernel(
    own_ref,
    k_ref, v_ref, n0_ref, d0_ref, n1_ref, d1_ref, n2_ref, d2_ref, s0_ref, s1_ref, s2_ref,
    kgrad_ref, vgrad_ref,
):
    strip = k_ref.shape[1]
    inv = 1.0 / (HEAD_DIM**0.5)
    at = lax.broadcasted_iota(jnp.int32, (strip, 1), 0)
    valid = (at >= own_ref[0]) & (at < own_ref[1])
    left = s1_ref[3:4, :] >= 1.5
    right_flags = s2_ref[3:4, :]
    right = (right_flags == 1.0) | (right_flags == 3.0)
    live = jnp.concatenate(
        [jnp.broadcast_to(valid, (strip, strip)), valid & left, valid & right], axis=1
    )
    normed, dout = (n0_ref, n1_ref, n2_ref), (d0_ref, d1_ref, d2_ref)
    each = range(2 * PER_STEP)
    scores = [dot(head(k_ref, i), heads_of(normed, i), NT) for i in each]
    dprob = [dot(head(v_ref, i), heads_of(dout, i), NT) for i in each]
    prob_b, dscore = [], []
    for i in each:
        rowmax, share, delta = (
            jnp.concatenate(
                [r[i * STATS + j : i * STATS + j + 1, :] for r in (s0_ref, s1_ref, s2_ref)], axis=1
            )
            for j in range(3)
        )
        masked = jnp.where(live, scores[i] * inv, DEAD)
        prob = jnp.exp(masked - rowmax) * share
        prob_b.append(prob.astype(jnp.bfloat16))
        dscore.append((prob * (dprob[i] - delta)).astype(jnp.bfloat16))
    for i in each:
        vgrad_ref[0, :, columns_of(i)] = dot(prob_b[i], heads_of(dout, i), NN).astype(jnp.bfloat16)
    for i in each:
        kgrad = dot(dscore[i], heads_of(normed, i), NN) * inv
        kgrad_ref[0, :, columns_of(i)] = kgrad.astype(jnp.bfloat16)


def total_over(blocks, axis, groups=None):
    if blocks.shape[0] > 1:
        blocks = lax.all_to_all(blocks, axis, 0, 0, axis_index_groups=groups, tiled=True)
    return jnp.sum(blocks, axis=0)


def copies(part, count):
    return jnp.broadcast_to(part[None], (count, *part.shape))


def tied(value, *others):
    return lax.optimization_barrier((value, *others))[0]


def on_device(queries, keys, values, out_grad, gain, tasks, bounds):
    _, strip, width = queries.shape
    heads = width // HEAD_DIM
    steps = heads // PER_STEP
    cols = PER_STEP * HEAD_DIM
    late_steps = max(steps // SHARE, 1)
    early_steps = steps - late_steps
    early_heads, late_width = early_steps * PER_STEP, late_steps * cols
    early_width = width - late_width
    n_dp = lax.axis_size("dp")
    count = lax.axis_size("view")
    ring = RING if count % RING == 0 else count

    def block(row, at=0, of=cols):
        return pl.BlockSpec((1, strip, of), lambda i: (0, row, at + i))

    whole = pl.BlockSpec((heads, HEAD_DIM), lambda i: (0, 0))
    scalars = pl.BlockSpec(memory_space=pltpu.SMEM)
    anywhere = pl.BlockSpec(memory_space=pl.ANY)
    wide = jax.ShapeDtypeStruct(queries.shape, jnp.bfloat16)
    own_bounds, own_tasks = bounds.reshape(2), tasks.reshape(2)
    mac = strip * strip * width

    def call(kernel, grid, in_specs, out_specs, out_shape, cost=0, aliases=None):
        run = pl.pallas_call(
            kernel,
            grid=(grid,),
            in_specs=in_specs,
            out_specs=out_specs,
            out_shape=out_shape,
            input_output_aliases=aliases or {},
            name=(kernel.func if isinstance(kernel, functools.partial) else kernel).__name__,
            compiler_params=pltpu.CompilerParams(vmem_limit_bytes=(63 if kernel is pack_kernel else 40) * 1024 * 1024),
            cost_estimate=pl.CostEstimate(flops=cost * mac, bytes_accessed=8 * strip * width, transcendentals=0),
        )
        return lambda *args: run(
            *(pltpu.with_memory_space_constraint(a, pltpu.VMEM) if kernel is key_kernel and a.size > 1 << 12 else a for a in args)
        )

    rows = 2 * strip + MASK_ROWS
    parts = PREP_STEPS
    thin, slim, part = early_width // parts, late_width // parts, width // parts
    kv0 = call(
        pack_kernel,
        parts,
        [scalars, block(0, 0, thin), block(0, 0, thin)],
        pl.BlockSpec((1, rows, thin), lambda i: (0, 0, i)),
        jax.ShapeDtypeStruct((1, rows, early_width), jnp.bfloat16),
    )(own_bounds, keys, values)
    kv0_left, kv0_right = shifted(kv0, "view", 1), shifted(kv0, "view", -1)
    late = block(0, early_width // slim, slim)
    kv1, nd = call(
        prep_kernel,
        parts,
        [late, late, block(0, 0, part), block(0, 0, part), whole],
        [
            pl.BlockSpec((1, 2 * strip, slim), lambda i: (0, 0, i)),
            pl.BlockSpec((1, 2 * strip, part), lambda i: (0, 0, i)),
        ],
        [
            jax.ShapeDtypeStruct((1, 2 * strip, late_width), jnp.bfloat16),
            jax.ShapeDtypeStruct((1, 2 * strip, width), jnp.bfloat16),
        ],
        cost=140,
    )(keys, values, queries, out_grad, gain)

    kv1_left, kv1_right = shifted(kv1, "view", 1), shifted(kv1, "view", -1)

    def query_side(half, left, right, before):
        near_args = [left, left, kv0_left, right, right, kv0_right]
        at = early_steps if half else 0
        mask = pl.BlockSpec((1, MASK_ROWS, strip), lambda i: (0, 2 * strip // MASK_ROWS, 0))
        near = [block(0), block(1), mask]
        count, per = (n_dp, heads) if half else (1, early_heads)
        return call(
            functools.partial(query_kernel, at * PER_STEP),
            late_steps if half else early_steps,
            [scalars] * 2 + [block(0, at)] * 5 + near * 2 + [whole]
            + [anywhere] * (3 if half else 0)
            + [pl.BlockSpec((1, early_heads, HEAD_DIM), lambda i: (0, 0, 0))] * (1 if half else 0),
            [
                block(0, at),
                block(0, at),
                pl.BlockSpec((PER_STEP * STATS, strip), lambda i: (at + i, 0)),
                pl.BlockSpec((count, per, HEAD_DIM), lambda i: (0, 0, 0)),
            ],
            [
                wide,
                wide,
                jax.ShapeDtypeStruct((heads * STATS, strip), jnp.float32),
                jax.ShapeDtypeStruct((count, per, HEAD_DIM), jnp.float32),
            ],
            cost=3000,
            aliases={14: 0, 15: 1, 16: 2} if half else None,
        )(
            own_tasks, own_bounds, queries, nd, out_grad, keys, values,
            *near_args, gain, *before,
        )

    kv0_right, kv0_left = lax.optimization_barrier((kv0_right, kv0_left))
    early = query_side(0, kv0_left, kv0_right, ())
    attended, qgrad, stats, gain_parts = query_side(1, kv1_left, kv1_right, early)
    nd_sent = tied(nd, early[3])
    nd_left, nd_right = shifted(nd_sent, "view", 1), shifted(nd_sent, "view", -1)
    nd_right, nd_left = lax.optimization_barrier((nd_right, nd_left))
    s_left, s_right = shifted(stats, "view", 1), shifted(stats, "view", -1)

    across = [[y * ring + z for y in range(count // ring)] for z in range(ring)]
    along = [[y * ring + z for z in range(ring)] for y in range(count // ring)]
    gain_grad = total_over(gain_parts, "dp")
    gain_grad = total_over(copies(gain_grad, count // ring), "view", across)

    both = 2 * cols
    own = [block(0, 0, both), block(1, 0, both)]
    stat_block = pl.BlockSpec((2 * PER_STEP * STATS, strip), lambda i: (i, 0))
    kgrad, vgrad = call(
        key_kernel,
        steps // 2,
        [scalars] + [block(0, 0, both)] * 2 + own * 3 + [stat_block] * 3,
        [block(0, 0, both)] * 2,
        [wide, wide],
        cost=30,
    )(
        own_bounds, keys, values, nd, nd, nd_left, nd_left, nd_right, nd_right, stats, s_left, s_right
    )
    blocks = lax.all_to_all(copies(gain_grad, ring), "view", 0, 0, axis_index_groups=along, tiled=True)
    gain_grad = jnp.sum(tied(blocks, kgrad), axis=0)
    return attended, qgrad, kgrad, vgrad, gain_grad


def solution(mesh):
    rows = P("dp", "view", None)
    return jax.shard_map(
        on_device,
        mesh=mesh,
        in_specs=(rows, rows, rows, rows, P(), rows, rows),
        out_specs=(rows, rows, rows, rows, P()),
        check_vma=False,
    )
```

```python
import functools

import jax
import jax.numpy as jnp
from jax import lax
from jax.experimental import pallas as pl
from jax.experimental.pallas import tpu as pltpu
from jax.sharding import PartitionSpec as P

HEAD_DIM = 128
DEAD = -1e30
EPS = 1e-06
PER_STEP = 4
STATS = 4
MASK_ROWS = 16
PREP_STEPS = 2
SHARE = 2
RING = 8
NT = (((1,), (1,)), ((), ()))
NN = (((1,), (0,)), ((), ()))


def dot(a, b, dims):
    return lax.dot_general(a, b, dims, preferred_element_type=jnp.float32)


def shifted(array, axis, by):
    count = lax.axis_size(axis)
    return lax.ppermute(array, axis, [(i, (i + by) % count) for i in range(count)])


def columns_of(i):
    return slice(i * HEAD_DIM, (i + 1) * HEAD_DIM)


def head(ref, i):
    return ref[0, :, columns_of(i)]


def heads_of(refs, i):
    return jnp.concatenate([head(r, i) for r in refs], axis=0)


def pack_kernel(own_ref, k_ref, v_ref, out_ref):
    strip, width = k_ref.shape[1:]
    out_ref[0, :strip, :] = k_ref[0]
    out_ref[0, strip : 2 * strip, :] = v_ref[0]
    at = lax.broadcasted_iota(jnp.int32, (MASK_ROWS, width), 1) % strip
    valid = (at >= own_ref[0]) & (at < own_ref[1])
    out_ref[0, 2 * strip :, :] = valid.astype(jnp.float32).astype(jnp.bfloat16)


def prep_kernel(k_ref, v_ref, k_all_ref, v_all_ref, q_ref, do_ref, gain_ref, kv_ref, nd_ref, own_ref):
    step = pl.program_id(0)
    strip = k_ref.shape[1]
    kv_ref[0, :strip, :] = k_ref[0]
    kv_ref[0, strip:, :] = v_ref[0]
    count = q_ref.shape[2] // HEAD_DIM
    for i in range(count):
        q = head(q_ref, i).astype(jnp.float32)
        gain = gain_ref[pl.ds(step * count + i, 1), :]
        scale = lax.rsqrt(jnp.mean(q * q, axis=-1, keepdims=True) + EPS)
        nd_ref[0, :strip, columns_of(i)] = (q * scale * gain).astype(jnp.bfloat16)
    nd_ref[0, strip:, :] = do_ref[0]
    own_ref[0, :strip, :] = k_all_ref[0]
    own_ref[0, strip:, :] = v_all_ref[0]


def query_kernel(
    start, tasks_ref, own_ref,
    q_ref, n_ref, do_ref, k0_ref, v0_ref, k1_ref, v1_ref, m1_ref, k2_ref, v2_ref, m2_ref, gain_ref,
    *rest,
):
    att_ref, qgrad_ref, stats_ref, gpart_ref = rest[-4:]
    if start:
        gpart_ref[:, :start, :] = jnp.broadcast_to(
            rest[3][...], (gpart_ref.shape[0], start, HEAD_DIM)
        )
    step = pl.program_id(0)
    strip = q_ref.shape[1]
    inv = 1.0 / (HEAD_DIM**0.5)
    at = lax.broadcasted_iota(jnp.int32, (1, strip), 1)
    flags = (tasks_ref[0] > 0).astype(jnp.float32), (tasks_ref[1] > 0).astype(jnp.float32)
    own = ((at >= own_ref[0]) & (at < own_ref[1])).astype(jnp.float32)
    left = m1_ref[0, 0:1, :].astype(jnp.float32) * flags[0]
    right = m2_ref[0, 0:1, :].astype(jnp.float32) * flags[1]
    live = jnp.concatenate([own, left, right], axis=1) > 0.5
    lane = lax.broadcasted_iota(jnp.int32, (strip, 128), 1)
    columns = jnp.full((strip, 128), flags[0] + 2.0 * flags[1], jnp.float32)
    keys, values = (k0_ref, k1_ref, k2_ref), (v0_ref, v1_ref, v2_ref)
    each = range(PER_STEP)
    scores = [dot(head(n_ref, i), heads_of(keys, i), NT) for i in each]
    dprob = [dot(head(do_ref, i), heads_of(values, i), NT) for i in each]
    prob_b, dscore = [], []
    for i in each:
        masked = jnp.where(live, scores[i] * inv, DEAD)
        rowmax = jnp.max(masked, axis=-1, keepdims=True)
        expo = jnp.exp(masked - rowmax)
        share = 1.0 / jnp.sum(expo, axis=-1, keepdims=True)
        prob = expo * share
        delta = jnp.sum(prob * dprob[i], axis=-1, keepdims=True)
        prob_b.append(prob.astype(jnp.bfloat16))
        dscore.append((prob * (dprob[i] - delta)).astype(jnp.bfloat16))
        for j, stat in enumerate((rowmax, share, delta)):
            columns = jnp.where(lane == i * STATS + j, stat, columns)
    dnormed = [dot(dscore[i], heads_of(keys, i), NN) * inv for i in each]
    for i in each:
        att_ref[0, :, columns_of(i)] = dot(prob_b[i], heads_of(values, i), NN).astype(jnp.bfloat16)
    for i in each:
        row = pl.ds(start + step * PER_STEP + i, 1)
        gain = gain_ref[row, :]
        q = head(q_ref, i).astype(jnp.float32)
        scale = lax.rsqrt(jnp.mean(q * q, axis=-1, keepdims=True) + EPS)
        inner = jnp.sum(q * gain * dnormed[i], axis=-1, keepdims=True)
        cubed = scale * scale * scale
        qgrad = gain * scale * dnormed[i] - q * (cubed * inner * (1.0 / HEAD_DIM))
        qgrad_ref[0, :, columns_of(i)] = qgrad.astype(jnp.bfloat16)
        part = jnp.sum(q * scale * dnormed[i], axis=0, keepdims=True)
        for j in range(gpart_ref.shape[0]):
            gpart_ref[j, row, :] = part
    stats_ref[...] = columns.T[: PER_STEP * STATS, :]


def key_kernel(
    own_ref,
    k_ref, v_ref, n0_ref, d0_ref, n1_ref, d1_ref, n2_ref, d2_ref, s0_ref, s1_ref, s2_ref,
    kgrad_ref, vgrad_ref,
):
    strip = k_ref.shape[1]
    inv = 1.0 / (HEAD_DIM**0.5)
    at = lax.broadcasted_iota(jnp.int32, (strip, 1), 0)
    valid = (at >= own_ref[0]) & (at < own_ref[1])
    left = s1_ref[3:4, :] >= 1.5
    right_flags = s2_ref[3:4, :]
    right = (right_flags == 1.0) | (right_flags == 3.0)
    live = jnp.concatenate(
        [jnp.broadcast_to(valid, (strip, strip)), valid & left, valid & right], axis=1
    )
    normed, dout = (n0_ref, n1_ref, n2_ref), (d0_ref, d1_ref, d2_ref)
    each = range(2 * PER_STEP)
    scores = [dot(head(k_ref, i), heads_of(normed, i), NT) for i in each]
    dprob = [dot(head(v_ref, i), heads_of(dout, i), NT) for i in each]
    prob_b, dscore = [], []
    for i in each:
        rowmax, share, delta = (
            jnp.concatenate(
                [r[i * STATS + j : i * STATS + j + 1, :] for r in (s0_ref, s1_ref, s2_ref)], axis=1
            )
            for j in range(3)
        )
        masked = jnp.where(live, scores[i] * inv, DEAD)
        prob = jnp.exp(masked - rowmax) * share
        prob_b.append(prob.astype(jnp.bfloat16))
        dscore.append((prob * (dprob[i] - delta)).astype(jnp.bfloat16))
    for i in each:
        vgrad_ref[0, :, columns_of(i)] = dot(prob_b[i], heads_of(dout, i), NN).astype(jnp.bfloat16)
    for i in each:
        kgrad = dot(dscore[i], heads_of(normed, i), NN) * inv
        kgrad_ref[0, :, columns_of(i)] = kgrad.astype(jnp.bfloat16)


def total_over(blocks, axis, groups=None):
    if blocks.shape[0] > 1:
        blocks = lax.all_to_all(blocks, axis, 0, 0, axis_index_groups=groups, tiled=True)
    return jnp.sum(blocks, axis=0)


def copies(part, count):
    return jnp.broadcast_to(part[None], (count, *part.shape))


def tied(value, *others):
    return lax.optimization_barrier((value, *others))[0]


def on_device(queries, keys, values, out_grad, gain, tasks, bounds):
    _, strip, width = queries.shape
    heads = width // HEAD_DIM
    steps = heads // PER_STEP
    cols = PER_STEP * HEAD_DIM
    late_steps = max(steps // SHARE, 1)
    early_steps = steps - late_steps
    early_heads, late_width = early_steps * PER_STEP, late_steps * cols
    early_width = width - late_width
    n_dp = lax.axis_size("dp")
    count = lax.axis_size("view")
    ring = RING if count % RING == 0 else count

    def block(row, at=0, of=cols):
        return pl.BlockSpec((1, strip, of), lambda i: (0, row, at + i))

    whole = pl.BlockSpec((heads, HEAD_DIM), lambda i: (0, 0))
    scalars = pl.BlockSpec(memory_space=pltpu.SMEM)
    anywhere = pl.BlockSpec(memory_space=pl.ANY)
    wide = jax.ShapeDtypeStruct(queries.shape, jnp.bfloat16)
    own_bounds, own_tasks = bounds.reshape(2), tasks.reshape(2)
    mac = strip * strip * width

    def call(kernel, grid, in_specs, out_specs, out_shape, cost=0, aliases=None):
        run = pl.pallas_call(
            kernel,
            grid=(grid,),
            in_specs=in_specs,
            out_specs=out_specs,
            out_shape=out_shape,
            input_output_aliases=aliases or {},
            name=(kernel.func if isinstance(kernel, functools.partial) else kernel).__name__,
            compiler_params=pltpu.CompilerParams(vmem_limit_bytes=(63 if kernel is pack_kernel else 40) * 1024 * 1024),
            cost_estimate=pl.CostEstimate(flops=cost * mac, bytes_accessed=8 * strip * width, transcendentals=0),
        )
        return lambda *args: run(
            *(pltpu.with_memory_space_constraint(a, pltpu.VMEM) if kernel is key_kernel and a.size > 1 << 12 else a for a in args)
        )

    rows = 2 * strip + MASK_ROWS
    parts = PREP_STEPS
    thin, slim, part = early_width // parts, late_width // parts, width // parts
    kv0 = call(
        pack_kernel,
        parts,
        [scalars, block(0, 0, thin), block(0, 0, thin)],
        pl.BlockSpec((1, rows, thin), lambda i: (0, 0, i)),
        jax.ShapeDtypeStruct((1, rows, early_width), jnp.bfloat16),
    )(own_bounds, keys, values)
    kv0_left, kv0_right = shifted(kv0, "view", 1), shifted(kv0, "view", -1)
    late = block(0, early_width // slim, slim)
    kv1, nd, kv_own = call(
        prep_kernel,
        parts,
        [late, late] + [block(0, 0, part)] * 4 + [whole],
        [
            pl.BlockSpec((1, 2 * strip, slim), lambda i: (0, 0, i)),
            pl.BlockSpec((1, 2 * strip, part), lambda i: (0, 0, i)),
            pl.BlockSpec((1, 2 * strip, part), lambda i: (0, 0, i)),
        ],
        [
            jax.ShapeDtypeStruct((1, 2 * strip, late_width), jnp.bfloat16),
            jax.ShapeDtypeStruct((1, 2 * strip, width), jnp.bfloat16),
            jax.ShapeDtypeStruct((1, 2 * strip, width), jnp.bfloat16),
        ],
        cost=140,
    )(keys, values, keys, values, queries, out_grad, gain)

    kv1_left, kv1_right = shifted(kv1, "view", 1), shifted(kv1, "view", -1)

    def query_side(half, left, right, before):
        near_args = [left, left, kv0_left, right, right, kv0_right]
        at = early_steps if half else 0
        mask = pl.BlockSpec((1, MASK_ROWS, strip), lambda i: (0, 2 * strip // MASK_ROWS, 0))
        near = [block(0), block(1), mask]
        count, per = (n_dp, heads) if half else (1, early_heads)
        return call(
            functools.partial(query_kernel, at * PER_STEP),
            late_steps if half else early_steps,
            [scalars] * 2 + [block(0, at)] * 5 + near * 2 + [whole]
            + [anywhere] * (3 if half else 0)
            + [pl.BlockSpec((1, early_heads, HEAD_DIM), lambda i: (0, 0, 0))] * (1 if half else 0),
            [
                block(0, at),
                block(0, at),
                pl.BlockSpec((PER_STEP * STATS, strip), lambda i: (at + i, 0)),
                pl.BlockSpec((count, per, HEAD_DIM), lambda i: (0, 0, 0)),
            ],
            [
                wide,
                wide,
                jax.ShapeDtypeStruct((heads * STATS, strip), jnp.float32),
                jax.ShapeDtypeStruct((count, per, HEAD_DIM), jnp.float32),
            ],
            cost=3000,
            aliases={14: 0, 15: 1, 16: 2} if half else None,
        )(
            own_tasks, own_bounds, queries, nd, out_grad, keys, values,
            *near_args, gain, *before,
        )

    kv0_right, kv0_left = lax.optimization_barrier((kv0_right, kv0_left))
    early = query_side(0, kv0_left, kv0_right, ())
    attended, qgrad, stats, gain_parts = query_side(1, kv1_left, kv1_right, early)
    nd_sent = tied(nd, early[3])
    nd_left, nd_right = shifted(nd_sent, "view", 1), shifted(nd_sent, "view", -1)
    nd_right, nd_left = lax.optimization_barrier((nd_right, nd_left))
    s_left, s_right = shifted(stats, "view", 1), shifted(stats, "view", -1)

    across = [[y * ring + z for y in range(count // ring)] for z in range(ring)]
    along = [[y * ring + z for z in range(ring)] for y in range(count // ring)]
    gain_grad = total_over(gain_parts, "dp")
    gain_grad = total_over(copies(gain_grad, count // ring), "view", across)

    both = 2 * cols
    own = [block(0, 0, both), block(1, 0, both)]
    stat_block = pl.BlockSpec((2 * PER_STEP * STATS, strip), lambda i: (i, 0))
    kgrad, vgrad = call(
        key_kernel,
        steps // 2,
        [scalars] + own * 4 + [stat_block] * 3,
        [block(0, 0, both)] * 2,
        [wide, wide],
        cost=30,
    )(
        own_bounds, kv_own, kv_own, nd, nd, nd_left, nd_left, nd_right, nd_right, stats, s_left, s_right
    )
    blocks = lax.all_to_all(copies(gain_grad, ring), "view", 0, 0, axis_index_groups=along, tiled=True)
    gain_grad = jnp.sum(tied(blocks, kgrad), axis=0)
    return attended, qgrad, kgrad, vgrad, gain_grad


def solution(mesh):
    rows = P("dp", "view", None)
    return jax.shard_map(
        on_device,
        mesh=mesh,
        in_specs=(rows, rows, rows, rows, P(), rows, rows),
        out_specs=(rows, rows, rows, rows, P()),
        check_vma=False,
    )
```
